256 devices in a mesh: section: 2 (over x_lo), dp: 4 (over y), mp: 32 (over z, x_hi, core).
Axes of the slice: x: 4 (x_hi: 2, x_lo: 2; x = x_hi * 2 + x_lo), y: 4, z: 8, core: 2. Of those that a mesh axis runs over, the one named last changes fastest.
Arguments:
- section_input: bfloat16 [2, 256, 8192], P('section', 'mp', 'dp')
- saved_input: bfloat16 [2, 256, 8192], P('section', 'mp', 'dp')
- cotangent: bfloat16 [2, 256, 8192], P('section', 'mp', 'dp'), may hold values from -6 to 6
- norm_gain: float32 [2, 8192], P('section', 'dp'), may hold values from 0.3 to 2.5
- norm_shift: float32 [2, 8192], P('section', 'dp'), may hold values from -3 to 3
- up_weight: bfloat16 [2, 8192, 16384], P('section', 'dp', 'mp'), may hold values from -0.0625 to 0.0625
- up_bias: float32 [2, 16384], P('section', 'mp'), may hold values from -3 to 3
- down_weight: bfloat16 [2, 16384, 8192], P('section', 'mp', 'dp'), may hold values from -0.046875 to 0.046875
- down_bias: float32 [2, 8192], P('section', 'dp'), may hold values from -3 to 3
Outputs:
- sent_forward: bfloat16 [2, 256, 8192], P('section', None, ('dp', 'mp'))
- sent_backward: bfloat16 [2, 256, 8192], P('section', None, ('dp', 'mp'))
- up_weight_grad: bfloat16 [2, 8192, 16384], P('section', 'dp', 'mp')
- up_bias_grad: float32 [2, 16384], P('section', 'mp')
- down_weight_grad: bfloat16 [2, 16384, 8192], P('section', 'mp', 'dp')
- down_bias_grad: float32 [2, 8192], P('section', 'dp')
- gain_grad: float32 [2, 8192], P('section', 'dp')
- shift_grad: float32 [2, 8192], P('section', 'dp')
The draws below stay inside these ranges and needn't reach their ends.
All inputs are finite; a program needn't handle non-finite values.
Results may differ from the reference program's by a relative error of at most 0.007.
Values may be sent and summed in bfloat16 or wider, within the bound.
No kernel may reach another device: no remote copies, remote signals or barrier semaphores. Data moves between devices by JAX's collectives and lax.ppermute only.
A program may use at most 64 MiB of HBM per device.

```python
import jax
import jax.numpy as jnp
from jax import lax

D = 8192
FF = 16384
TOK = 256
SECTIONS = 2


def layout_scale(key_cols, key_rows, reach):
    ramp = jnp.linspace(-reach, reach, D, dtype=jnp.float32)[None, None, :]
    rough = jax.random.uniform(key_cols, (SECTIONS, 1, D), jnp.float32, -0.4, 0.4)
    column_scale = jnp.exp(ramp + rough)
    row_scale = jnp.exp(jax.random.uniform(key_rows, (SECTIONS, TOK, 1), jnp.float32, -1.15, 1.15))
    return column_scale * row_scale * 0.5


def draw_section_input(key, part):
    key = jax.random.fold_in(key, 11)
    keys = jax.random.split(key, 3)
    scale = layout_scale(keys[0], keys[1], 1.15)
    noise = jax.random.normal(keys[2], (SECTIONS, TOK, D), jnp.float32)
    return (jnp.clip(noise, -5.0, 5.0) * scale).astype(jnp.bfloat16)


def draw_saved_input(key, part):
    key = jax.random.fold_in(key, 23)
    keys = jax.random.split(key, 3)
    scale = layout_scale(keys[0], keys[1], 1.15)
    noise = jax.random.normal(keys[2], (SECTIONS, TOK, D), jnp.float32)
    return (jnp.clip(noise, -5.0, 5.0) * scale).astype(jnp.bfloat16)


def draw_norm_gain(key, part):
    key = jax.random.fold_in(key, 37)
    ramp = jnp.linspace(0.4, 1.6, D, dtype=jnp.float32)[None, :]
    rough = jax.random.uniform(key, (SECTIONS, D), jnp.float32, 0.8, 1.2)
    return jnp.clip(ramp * rough, 0.3, 2.5).astype(jnp.float32)


def levels(rng, shape, shards, least, largest):
    level, own = 1.0, jax.random.fold_in(rng, 6)
    for position, blocks in shards:
        steps = jnp.exp(jax.random.uniform(jax.random.fold_in(own, position), (blocks,), jnp.float32, least / len(shards), largest / len(shards)))
        level = level * jnp.repeat(steps, shape[position] // blocks).reshape([-1 if axis == position else 1 for axis in range(len(shape))])
    return level


def bell_draw(own_key, dims, scale, most, cuts=(), kind=jnp.bfloat16):
    factor_of = levels(own_key, dims, cuts, -0.22, 0.18) if cuts else 1.0
    result = jax.random.normal(own_key, dims, jnp.float32) * scale * factor_of
    return jnp.minimum(jnp.maximum(result, -most), most).astype(kind)


def setup_inputs(seed: int = 0) -> dict:
    arg_keys = jax.random.split(jax.random.key(seed), 10)
    section_input = draw_section_input(jax.random.fold_in(arg_keys[9], 71), 0)
    saved_input = draw_saved_input(jax.random.fold_in(arg_keys[9], 71), 0)
    cotangent = bell_draw(arg_keys[2], (SECTIONS, TOK, D), 1.0, 6.0, ((0, 2), (1, 32), (2, 4)))
    norm_gain = draw_norm_gain(jax.random.fold_in(arg_keys[9], 71), 0)
    norm_shift = bell_draw(arg_keys[4], (SECTIONS, D), 0.5, 3.0, ((0, 2), (1, 4)), jnp.float32)
    up_weight = bell_draw(arg_keys[5], (SECTIONS, D, FF), D ** -0.5, 0.0625, ((0, 2), (1, 4), (2, 32)))
    up_bias = bell_draw(arg_keys[6], (SECTIONS, FF), 0.5, 3.0, ((0, 2), (1, 32)), jnp.float32)
    down_weight = bell_draw(arg_keys[7], (SECTIONS, FF, D), FF ** -0.5, 0.046875, ((0, 2), (1, 32), (2, 4)))
    down_bias = bell_draw(arg_keys[8], (SECTIONS, D), 0.5, 3.0, ((0, 2), (1, 4)), jnp.float32)
    return {"section_input": section_input, "saved_input": saved_input, "cotangent": cotangent, "norm_gain": norm_gain, "norm_shift": norm_shift, "up_weight": up_weight, "up_bias": up_bias, "down_weight": down_weight, "down_bias": down_bias}


EPS = 1e-05
COEF_A = 0.7978845608028654
COEF_B = 0.044715

def gelu_value(value):
    inner = jnp.tanh(COEF_A * (value + COEF_B * value * value * value))
    return 0.5 * value * (1.0 + inner)

def gelu_slope(value):
    inner = jnp.tanh(COEF_A * (value + COEF_B * value * value * value))
    return 0.5 * (1.0 + inner) + 0.5 * value * (1.0 - inner * inner) * COEF_A * (1.0 + 3.0 * COEF_B * value * value)

def normalize(rows, gain, shift):
    values = rows.astype(jnp.float32)
    mean_row = lax.optimization_barrier(jnp.sum(values, 1, keepdims=True)) / D
    square_row = lax.optimization_barrier(jnp.sum(values * values, 1, keepdims=True)) / D
    rstd_row = lax.rsqrt(square_row - mean_row * mean_row + EPS)
    centered = (values - mean_row) * rstd_row
    normed = (centered * gain + shift).astype(jnp.bfloat16)
    return (normed, centered, rstd_row)

def reference(section_input, saved_input, cotangent, norm_gain, norm_shift, up_weight, up_bias, down_weight, down_bias):
    outputs, input_grads = ([], [])
    up_grads, up_bias_grads, down_grads, down_bias_grads, gain_grads, shift_grads = ([], [], [], [], [], [])
    for section in range(SECTIONS):
        gain, shift = (norm_gain[section], norm_shift[section])
        w_up, w_down = (up_weight[section], down_weight[section])
        normed, _, _ = normalize(section_input[section], gain, shift)
        pre = jnp.dot(normed, w_up, preferred_element_type=jnp.float32) + up_bias[section]
        activated = gelu_value(pre).astype(jnp.bfloat16)
        branch = jnp.dot(activated, w_down, preferred_element_type=jnp.float32)
        outputs.append((section_input[section].astype(jnp.float32) + branch + down_bias[section]).astype(jnp.bfloat16))
        normed, centered, rstd_row = normalize(saved_input[section], gain, shift)
        pre = jnp.dot(normed, w_up, preferred_element_type=jnp.float32) + up_bias[section]
        activated = gelu_value(pre).astype(jnp.bfloat16)
        grad_out = cotangent[section]
        back = jnp.dot(grad_out, w_down.T, preferred_element_type=jnp.float32)
        grad_pre = (back * gelu_slope(pre)).astype(jnp.bfloat16)
        down_grads.append(jnp.dot(activated.T, grad_out, preferred_element_type=jnp.float32).astype(jnp.bfloat16))
        down_bias_grads.append(lax.optimization_barrier(jnp.sum(grad_out.astype(jnp.float32), 0)))
        up_grads.append(jnp.dot(normed.T, grad_pre, preferred_element_type=jnp.float32).astype(jnp.bfloat16))
        up_bias_grads.append(lax.optimization_barrier(jnp.sum(grad_pre.astype(jnp.float32), 0)))
        grad_normed = jnp.dot(grad_pre, w_up.T, preferred_element_type=jnp.float32)
        gain_grads.append(lax.optimization_barrier(jnp.sum(grad_normed * centered, 0)))
        shift_grads.append(lax.optimization_barrier(jnp.sum(grad_normed, 0)))
        scaled = grad_normed * gain
        first = lax.optimization_barrier(jnp.sum(scaled, 1, keepdims=True)) / D
        second = lax.optimization_barrier(jnp.sum(scaled * centered, 1, keepdims=True)) / D
        grad_in = grad_out.astype(jnp.float32) + rstd_row * (scaled - first - centered * second)
        input_grads.append(grad_in.astype(jnp.bfloat16))
    sent_forward = jnp.roll(jnp.stack(outputs), 1, axis=0)
    sent_backward = jnp.roll(jnp.stack(input_grads), -1, axis=0)
    return (sent_forward, sent_backward, jnp.stack(up_grads), jnp.stack(up_bias_grads), jnp.stack(down_grads), jnp.stack(down_bias_grads), jnp.stack(gain_grads), jnp.stack(shift_grads))
```

```python
import jax
import jax.numpy as jnp
from jax import lax
from jax.sharding import Mesh, PartitionSpec as P

D = 8192


EPS = 1e-05
COEF_A = 0.7978845608028654
COEF_B = 0.044715
F32 = jnp.float32
BF = jnp.bfloat16


def shifted(value, axis, steps):
    count = lax.axis_size(axis)
    return lax.ppermute(value, axis, [(i, (i + steps) % count) for i in range(count)])


def swapped(value, axis, bit):
    count = lax.axis_size(axis)
    return lax.ppermute(value, axis, [(i, i ^ bit) for i in range(count)])


def gelu_value(value):
    inner = jnp.tanh(COEF_A * (value + COEF_B * value * value * value))
    return 0.5 * value * (1.0 + inner)


def gelu_slope(value):
    inner = jnp.tanh(COEF_A * (value + COEF_B * value * value * value))
    return 0.5 * (1.0 + inner) + 0.5 * value * (1.0 - inner * inner) * COEF_A * (
        1.0 + 3.0 * COEF_B * value * value
    )


def paired(mine, axis, place):
    other = swapped(mine, axis, 1)
    first = lax.axis_index(axis) == 0
    return jnp.where(
        first, jnp.stack([mine, other], place), jnp.stack([other, mine], place)
    )


def gather_tokens(own):
    ahead, behind = [own], [own]
    for _ in range(4):
        ahead.append(shifted(ahead[-1], "z", 1))
    for _ in range(3):
        behind.append(shifted(behind[-1], "z", -1))
    around = jnp.stack([own] + behind[1:] + [ahead[4], ahead[3], ahead[2], ahead[1]], 1)
    column = jnp.roll(around, lax.axis_index("z"), axis=1)
    plane = paired(column, "xh", 2)
    whole = paired(plane, "core", 3)
    return whole.reshape(own.shape[0], -1, own.shape[2])


def take(value, index, axis):
    return lax.dynamic_index_in_dim(value, index, axis, keepdims=False)


def local(
    section_input,
    saved_input,
    cotangent,
    norm_gain,
    norm_shift,
    up_weight,
    up_bias,
    down_weight,
    down_bias,
):
    gain, shift = (norm_gain[0], norm_shift[0])
    w_up, w_down = (up_weight[0], down_weight[0])
    bias_up, bias_down = (up_bias[0], down_bias[0])
    at_z, at_h, at_c = (lax.axis_index("z"), lax.axis_index("xh"), lax.axis_index("core"))
    piece = 64
    start_column = (at_z * 4 + at_h * 2 + at_c) * piece

    own = jnp.stack([section_input[0], saved_input[0], cotangent[0]])
    gathered = gather_tokens(own)
    grad_full = gathered[2]

    partial_back = lax.dot_general(
        grad_full, w_down, (((1,), (1,)), ((), ())), preferred_element_type=F32
    )
    values = gathered[:2].astype(F32)
    sums = jnp.stack([jnp.sum(values, 2), jnp.sum(values * values, 2)])
    sums = sums + shifted(sums, "dp", 1) + shifted(sums, "dp", 2) + shifted(sums, "dp", 3)
    mean = sums[0] / D
    rstd = lax.rsqrt(sums[1] / D - mean * mean + EPS)
    centered = (values - mean[:, :, None]) * rstd[:, :, None]
    normed = (centered * gain + shift).astype(BF)
    partial_pre = jnp.dot(normed.reshape(-1, normed.shape[2]), w_up, preferred_element_type=F32)

    parts = jnp.concatenate([partial_pre.astype(BF), partial_back.astype(BF)])
    parts = parts.reshape(3, 4, 64, 512).transpose(1, 0, 2, 3)
    parts = lax.all_to_all(parts, "dp", 0, 0, tiled=False)
    total = jnp.sum(parts.astype(F32), 0)
    pre = total[:2] + bias_up
    act = gelu_value(pre).astype(BF)
    grad_pre = (total[2] * gelu_slope(pre[1])).astype(BF)
    quarter = jnp.concatenate([act, grad_pre[None]])
    hops = [shifted(quarter, "dp", -k) for k in (1, 2, 3)]
    hidden = jnp.roll(jnp.stack([quarter] + hops, 1), lax.axis_index("dp"), axis=1)
    hidden = hidden.reshape(3, 256, 512)
    act_forward, act_saved, grad_pre = hidden[0], hidden[1], hidden[2]

    forward_t = lax.dot_general(
        w_down, act_forward, (((0,), (1,)), ((), ())), preferred_element_type=F32
    )
    normed_t = lax.dot_general(
        w_up, grad_pre, (((1,), (1,)), ((), ())), preferred_element_type=F32
    )
    forward_t = forward_t.reshape(8, 2, 2, piece, 256)
    normed_t = normed_t.reshape(8, 2, 2, piece, 256)

    def both(index, axis, a, b):
        return jnp.stack([take(a, index, axis), take(b, index, axis)], axis)

    kept = both(at_c, 2, forward_t, normed_t)
    given = both(1 - at_c, 2, forward_t, normed_t).astype(BF)
    kept = kept + swapped(given, "core", 1).astype(F32)
    given = take(kept, 1 - at_h, 1).astype(BF)
    kept = take(kept, at_h, 1) + swapped(given, "xh", 1).astype(F32)
    blocks = lax.all_to_all(kept.astype(BF), "z", 0, 0, tiled=False)
    columns = jnp.sum(blocks.astype(F32), 0)

    grad_normed = lax.dot_general(
        grad_pre, w_up, (((1,), (1,)), ((), ())), preferred_element_type=F32
    )
    scaled = grad_normed * gain
    moments = jnp.stack([jnp.sum(scaled, 1), jnp.sum(scaled * centered[1], 1)])
    params = jnp.stack([jnp.sum(grad_normed * centered[1], 0), jnp.sum(grad_normed, 0)])
    moments = (
        moments
        + shifted(moments, "dp", 1)
        + shifted(moments, "dp", 2)
        + shifted(moments, "dp", 3)
    )
    small = jnp.concatenate([moments, params], 1)
    for axis, bit in (("core", 1), ("xh", 1), ("z", 1), ("z", 2), ("z", 4)):
        small = small + swapped(small, axis, bit)
    moments, params = small[:, :256], small[:, 256:]

    def own_columns(value):
        return lax.dynamic_slice_in_dim(value, start_column, piece, 1).astype(F32).T

    def own_piece(vector):
        return lax.dynamic_slice_in_dim(vector, start_column, piece, 0)[:, None]

    out = (own_columns(gathered[0]) + columns[0] + own_piece(bias_down)).astype(BF)
    forward_arrived = shifted(out.T, "section", 1)

    centered_columns = (own_columns(gathered[1]) - mean[1]) * rstd[1]
    grad_in = own_columns(grad_full) + rstd[1] * (
        columns[1] * own_piece(gain) - moments[0] / D - centered_columns * (moments[1] / D)
    )
    backward_arrived = shifted(grad_in.astype(BF).T, "section", -1)

    down_weight_grad = lax.dot_general(
        act_saved, grad_full, (((0,), (0,)), ((), ())), preferred_element_type=F32
    ).astype(BF)
    down_bias_grad = jnp.sum(grad_full.astype(F32), 0)
    up_weight_grad = lax.dot_general(
        normed[1], grad_pre, (((0,), (0,)), ((), ())), preferred_element_type=F32
    ).astype(BF)
    up_bias_grad = jnp.sum(grad_pre.astype(F32), 0)
    return (
        forward_arrived[None],
        backward_arrived[None],
        up_weight_grad[None],
        up_bias_grad[None],
        down_weight_grad[None],
        down_bias_grad[None],
        params[0][None],
        params[1][None],
    )


def solution(mesh):
    names = ("section", "dp", "z", "xh", "core")
    split = Mesh(mesh.devices.reshape(2, 4, 8, 2, 2), names)
    mp = ("z", "xh", "core")
    placed = (
        P("section", mp, "dp"),
        P("section", mp, "dp"),
        P("section", mp, "dp"),
        P("section", "dp"),
        P("section", "dp"),
        P("section", "dp", mp),
        P("section", mp),
        P("section", mp, "dp"),
        P("section", "dp"),
    )
    return jax.shard_map(
        local,
        mesh=split,
        in_specs=placed,
        out_specs=(
            P("section", None, ("dp",) + mp),
            P("section", None, ("dp",) + mp),
            P("section", "dp", mp),
            P("section", mp),
            P("section", mp, "dp"),
            P("section", "dp"),
            P("section", "dp"),
            P("section", "dp"),
        ),
        check_vma=False,
    )
```

```python
import jax
import jax.numpy as jnp
from jax import lax
from jax.experimental import pallas as pl
from jax.experimental.pallas import tpu as pltpu
from jax.sharding import Mesh, PartitionSpec as P

D = 8192


EPS = 1e-05
COEF_A = 0.7978845608028654
COEF_B = 0.044715
F32 = jnp.float32
BF = jnp.bfloat16


def shifted(value, axis, steps):
    count = lax.axis_size(axis)
    return lax.ppermute(value, axis, [(i, (i + steps) % count) for i in range(count)])


def swapped(value, axis, bit):
    count = lax.axis_size(axis)
    return lax.ppermute(value, axis, [(i, i ^ bit) for i in range(count)])


def gelu_value(value):
    inner = jnp.tanh(COEF_A * (value + COEF_B * value * value * value))
    return 0.5 * value * (1.0 + inner)


def gelu_slope(value):
    inner = jnp.tanh(COEF_A * (value + COEF_B * value * value * value))
    return 0.5 * (1.0 + inner) + 0.5 * value * (1.0 - inner * inner) * COEF_A * (
        1.0 + 3.0 * COEF_B * value * value
    )


def take(value, index, axis):
    return lax.dynamic_index_in_dim(value, index, axis, keepdims=False)


def over_dp(value):
    return value + shifted(value, "dp", 1) + shifted(value, "dp", 2) + shifted(value, "dp", 3)


def gather_half(own):
    at_z, even = lax.axis_index("z"), lax.axis_index("xh") == 0
    other = swapped(own, "xh", 1)
    pair = jnp.where(even, jnp.stack([own, other], 1), jnp.stack([other, own], 1))
    whole = jnp.zeros((own.shape[0], 8) + pair.shape[1:], own.dtype)
    whole = lax.dynamic_update_index_in_dim(whole, pair, at_z, 1)
    ahead, behind = pair, pair
    for step in range(1, 5):
        ahead = shifted(ahead, "z", 1)
        if step < 4:
            behind = shifted(behind, "z", -1)
            whole = lax.dynamic_update_index_in_dim(whole, behind, (at_z + step) % 8, 1)
        whole = lax.dynamic_update_index_in_dim(whole, ahead, (at_z + 8 - step) % 8, 1)
    return whole.reshape(own.shape[0], 128, own.shape[2])


def together_kernel(a, b, c, whole):
    for i, part in enumerate((a, b, c)):
        whole[i] = part[0]


def together(a, b, c):
    return pl.pallas_call(
        together_kernel,
        out_shape=jax.ShapeDtypeStruct((3,) + a.shape[1:], a.dtype),
        name="together",
    )(a, b, c)


def in_thirds(value):
    high = value.astype(BF).astype(F32)
    rest = value - high
    middle = rest.astype(BF).astype(F32)
    return high, middle, rest - middle


def entry_kernel(mine, other, gain, shift, w_up, w_down, sent, scaled, grads, rows, extra, turned):
    width = mine.shape[2]
    extra[...] = jnp.zeros_like(extra)
    rows[...] = jnp.zeros_like(rows)
    lane = lax.broadcasted_iota(jnp.int32, (128, 128), 1)
    for half, tokens in enumerate((mine, other)):
        columns = jnp.zeros((128, 128), F32)
        for i in range(2):
            value = tokens[i].astype(F32)
            total = jnp.sum(value, 1, keepdims=True)
            square = jnp.sum(value * value, 1, keepdims=True)
            columns = jnp.where(lane == 2 * i, total, columns)
            columns = jnp.where(lane == 2 * i + 1, square, columns)
            scaled[i, half * 128 : half * 128 + 128, :] = (
                (value - total / width) * gain[...]
            ).astype(BF)
        turned[...] = columns.T
        grads[half * 128 : half * 128 + 128, :] = tokens[2]
        for k, third in enumerate(in_thirds(turned[0:4, :])):
            extra[6 + 4 * half : 10 + 4 * half, k * 128 : k * 128 + 128] = third
    for j, vector in enumerate((gain, shift)):
        for k, third in enumerate(in_thirds(vector[...])):
            rows[3 * j + k : 3 * j + k + 1, :] = third
    sums = jnp.dot(rows[...].astype(BF), w_up[...], preferred_element_type=F32)
    for j in range(2):
        vector = sums[3 * j : 3 * j + 1] + sums[3 * j + 1 : 3 * j + 2] + sums[3 * j + 2 : 3 * j + 3]
        for k, third in enumerate(in_thirds(vector)):
            extra[3 * j + k : 3 * j + k + 1, :] = third
    for i in range(2):
        product = jnp.dot(scaled[i], w_up[...], preferred_element_type=F32).astype(BF)
        for q in range(4):
            sent[q, 64 * i : 64 * i + 64, :] = product[64 * q : 64 * q + 64]
    back = lax.dot_general(
        grads[...], w_down[...], (((1,), (1,)), ((), ())), preferred_element_type=F32
    ).astype(BF)
    for q in range(4):
        sent[q, 128:192, :] = back[64 * q : 64 * q + 64]
        sent[q, 192:208, :] = extra[...].astype(BF)


def entry(mine, other, gain, shift, w_up, w_down):
    return pl.pallas_call(
        entry_kernel,
        in_specs=[pl.BlockSpec(memory_space=pltpu.VMEM)] * 6,
        out_specs=pl.BlockSpec(memory_space=pltpu.VMEM),
        out_shape=jax.ShapeDtypeStruct((4, 208, 512), BF),
        scratch_shapes=[
            pltpu.VMEM((2, 256, 2048), BF),
            pltpu.VMEM((256, 2048), BF),
            pltpu.VMEM((8, 2048), F32),
            pltpu.VMEM((16, 512), F32),
            pltpu.VMEM((128, 128), F32),
        ],
        compiler_params=pltpu.CompilerParams(vmem_limit_bytes=28 * 2**20),
        cost_estimate=pl.CostEstimate(
            flops=2**31, bytes_accessed=8 * 2**20, transcendentals=0
        ),
        name="entry",
    )(mine, other, gain, shift, w_up, w_down)


def middle_kernel(at_dp, parts, bias, quarter, stats, rows):
    extra = parts[:, 192:208, :].astype(F32)
    weights = [
        [extra[y, 3 * j : 3 * j + 1] + extra[y, 3 * j + 1 : 3 * j + 2] + extra[y, 3 * j + 2 : 3 * j + 3] for y in range(4)]
        for j in range(2)
    ]
    offset = weights[1][0] + weights[1][1] + weights[1][2] + weights[1][3] + bias[...]
    rows[...] = jnp.zeros_like(rows)
    for half in range(2):
        block = extra[:, 6 + 4 * half : 10 + 4 * half, :]
        sums = block[:, :, 0:128] + block[:, :, 128:256] + block[:, :, 256:384]
        whole = sums[0] + sums[1] + sums[2] + sums[3]
        for i in range(2):
            mean = whole[2 * i : 2 * i + 1] / D
            square = whole[2 * i + 1 : 2 * i + 2] / D
            rows[2 * i : 2 * i + 1, :] = mean
            rows[2 * i + 1 : 2 * i + 2, :] = lax.rsqrt(square - mean * mean + EPS)
            for y in range(4):
                at = 4 + 4 * i + y
                rows[at : at + 1, :] = sums[y, 2 * i : 2 * i + 1] / (D // 4) - mean
        stats[half * 128 : half * 128 + 128, :] = rows[...].T
    own = stats[pl.ds(pl.multiple_of(at_dp[0] * 64, 64), 64), :]
    for i in range(2):
        total = jnp.zeros((64, 512), F32)
        for y in range(4):
            at = 4 + 4 * i + y
            total += parts[y, 64 * i : 64 * i + 64, :].astype(F32)
            total += own[:, at : at + 1] * weights[0][y]
        pre = own[:, 2 * i + 1 : 2 * i + 2] * total + offset
        quarter[i] = gelu_value(pre).astype(BF)
    back = parts[0, 128:192, :].astype(F32)
    for y in range(1, 4):
        back += parts[y, 128:192, :].astype(F32)
    quarter[2] = (back * gelu_slope(pre)).astype(BF)


def middle(parts, bias):
    return pl.pallas_call(
        middle_kernel,
        in_specs=[pl.BlockSpec(memory_space=pltpu.SMEM)]
        + [pl.BlockSpec(memory_space=pltpu.VMEM)] * 2,
        out_specs=[pl.BlockSpec(memory_space=pltpu.VMEM)] * 2,
        out_shape=[
            jax.ShapeDtypeStruct((3, 64, 512), BF),
            jax.ShapeDtypeStruct((256, 128), F32),
        ],
        scratch_shapes=[pltpu.VMEM((128, 128), F32)],
        compiler_params=pltpu.CompilerParams(vmem_limit_bytes=12 * 2**20),
        cost_estimate=pl.CostEstimate(
            flops=2**22, bytes_accessed=2**20, transcendentals=2**17
        ),
        name="middle",
    )(lax.axis_index("dp").reshape(1), parts, bias)


def products_kernel(
    at_dp, own, next1, next2, next3, w_up, w_down, mine, other, stats, gain,
    kept, given, hidden, bias_grad, params, moments, plain, crossed,
):
    step = pl.program_id(0)

    @pl.when(step == 0)
    def _():
        for k, quarter in enumerate((own, next1, next2, next3)):
            row = pl.multiple_of(((at_dp[0] + k) % 4) * 64, 64)
            for i in range(3):
                hidden[i, pl.ds(row, 64), :] = quarter[i]
        bias_grad[...] = jnp.sum(hidden[2].astype(F32), 0, keepdims=True)
        plain[...] = jnp.zeros_like(plain)
        crossed[...] = jnp.zeros_like(crossed)

    branch = jnp.dot(hidden[0], w_down[...], preferred_element_type=F32)
    back = lax.dot_general(
        hidden[2], w_up[...], (((1,), (1,)), ((), ())), preferred_element_type=F32
    )
    for h in range(2):
        lanes = slice(h * 128, h * 128 + 128)
        for i, product in enumerate((branch, back)):
            kept[0, h, i] = product[:128, lanes]
            given[0, h, i] = product[128:, lanes].astype(BF)
    saved = jnp.concatenate([mine[0], other[0]]).astype(F32)
    centered = (saved - stats[:, 2:3]) * stats[:, 3:4]
    crossing = back * centered
    params[0:1, :] = jnp.sum(crossing, 0, keepdims=True)
    params[1:2, :] = jnp.sum(back, 0, keepdims=True)
    plain[...] += back * gain[...]
    crossed[...] += crossing * gain[...]

    @pl.when(step == 7)
    def _():
        ones = jnp.ones((8, 256), F32)
        for i, total in enumerate((plain, crossed)):
            row = lax.dot_general(
                ones, total[...], (((1,), (1,)), ((), ())),
                precision=lax.Precision.HIGHEST, preferred_element_type=F32,
            )
            moments[i : i + 1, :] = row[0:1]


def products(quarters, w_up, w_down, mine, other, stats, gain):
    whole = lambda *shape: pl.BlockSpec(shape, lambda i: (0,) * len(shape))
    out = lambda shape, kind: jax.ShapeDtypeStruct(shape, kind)
    return pl.pallas_call(
        products_kernel,
        grid=(8,),
        in_specs=[pl.BlockSpec(memory_space=pltpu.SMEM)]
        + [whole(3, 64, 512)] * 4
        + [
            pl.BlockSpec((256, 512), lambda i: (i, 0)),
            pl.BlockSpec((512, 256), lambda i: (0, i)),
            pl.BlockSpec((1, 128, 256), lambda i: (1, 0, i)),
            pl.BlockSpec((1, 128, 256), lambda i: (1, 0, i)),
            whole(256, 128),
            pl.BlockSpec((1, 256), lambda i: (0, i)),
        ],
        out_specs=[
            pl.BlockSpec((1, 2, 2, 128, 128), lambda i: (i, 0, 0, 0, 0)),
            pl.BlockSpec((1, 2, 2, 128, 128), lambda i: (i, 0, 0, 0, 0)),
            whole(3, 256, 512),
            whole(1, 512),
            pl.BlockSpec((2, 256), lambda i: (0, i)),
            whole(2, 256),
        ],
        out_shape=[
            out((8, 2, 2, 128, 128), F32),
            out((8, 2, 2, 128, 128), BF),
            out((3, 256, 512), BF),
            out((1, 512), F32),
            out((2, 2048), F32),
            out((2, 256), F32),
        ],
        scratch_shapes=[pltpu.VMEM((256, 256), F32)] * 2,
        compiler_params=pltpu.CompilerParams(vmem_limit_bytes=12 * 2**20),
        cost_estimate=pl.CostEstimate(
            flops=2**31, bytes_accessed=10 * 2**20, transcendentals=0
        ),
        name="products",
    )(lax.axis_index("dp").reshape(1), *quarters, w_up, w_down, mine, other, stats, gain)


def relayed(tiles):
    count = tiles.shape[0]
    even = lax.axis_index("core") == 0
    low, high = tiles[:, :, :64], tiles[:, :, 64:]
    same = swapped(jnp.where(even, low, high), "section", 1)
    cross = lax.ppermute(jnp.where(even, high, low), ("section", "core"), [(i, 3 - i) for i in range(4)])
    same, cross = same.reshape(count, 16, 8, 64), cross.reshape(count, 16, 8, 64)
    joined = jnp.where(even, jnp.stack([same, cross], 2), jnp.stack([cross, same], 2))
    return joined.reshape(count, 256, 64)


def local(
    section_input,
    saved_input,
    cotangent,
    norm_gain,
    norm_shift,
    up_weight,
    up_bias,
    down_weight,
    down_bias,
):
    gain, shift = (norm_gain[0], norm_shift[0])
    w_up, w_down = (up_weight[0], down_weight[0])
    bias_up, bias_down = (up_bias[0], down_bias[0])
    at_z, at_h = (lax.axis_index("z"), lax.axis_index("xh"))
    first_column = at_z * 256 + at_h * 128

    mine = gather_half(together(section_input, saved_input, cotangent))
    other = swapped(mine, "core", 1)

    parts = entry(mine, other, gain[None], shift[None], w_up, w_down)
    parts = lax.all_to_all(parts, "dp", 0, 0, tiled=False)
    quarter, stats = middle(parts, bias_up[None])
    quarters = [quarter] + [shifted(quarter, "dp", -k) for k in (1, 2, 3)]

    kept, given, hidden, bias_grad, params, moments = products(
        quarters, w_up, w_down, mine, other, stats, gain[None]
    )
    summed = kept + swapped(given, "core", 1).astype(F32)
    given = take(summed, 1 - at_h, 1).astype(BF)
    small = jnp.concatenate([moments, params], 1)
    kept = take(summed, at_h, 1) + swapped(given, "xh", 1).astype(F32)
    for bit in (1, 2, 4):
        small = small + swapped(small, "z", bit)
    tiles = jnp.sum(lax.all_to_all(kept.astype(BF), "z", 0, 0, tiled=False).astype(F32), 0)
    small = jnp.concatenate([small[:, :128], small[:, 256:]], 1) + swapped(
        small[:, 128:], "core", 1
    )
    small = small + swapped(small, "xh", 1)
    small = jnp.concatenate([over_dp(small[:, :128]), small[:, 128:]], 1)
    moments, params = small[:, :128], small[:, 128:]

    def own_tile(value):
        return lax.dynamic_slice_in_dim(value, first_column, 128, 1).astype(F32)

    def own_columns(vector):
        return lax.dynamic_slice_in_dim(vector, first_column, 128, 0)

    out = (own_tile(mine[0]) + tiles[0] + own_columns(bias_down)).astype(BF)

    rstd_rows = stats[:128, 3:4]
    centered_tile = (own_tile(mine[1]) - stats[:128, 2:3]) * rstd_rows
    first, second = moments[0][:, None] / D, moments[1][:, None] / D
    grad_in = own_tile(mine[2]) + rstd_rows * (
        tiles[1] * own_columns(gain) - first - centered_tile * second
    )
    arrived = relayed(jnp.stack([out, grad_in.astype(BF)]))

    grad_full = jnp.concatenate([mine[2], other[2]])
    saved = jnp.concatenate([mine[1], other[1]]).astype(F32)
    normed = ((saved - stats[:, 2:3]) * stats[:, 3:4] * gain + shift).astype(BF)
    down_weight_grad = lax.dot_general(
        hidden[1], grad_full, (((0,), (0,)), ((), ())), preferred_element_type=F32
    ).astype(BF)
    down_bias_grad = jnp.sum(grad_full.astype(F32), 0)
    up_weight_grad = lax.dot_general(
        normed, hidden[2], (((0,), (0,)), ((), ())), preferred_element_type=F32
    ).astype(BF)
    return (
        arrived[0][None],
        arrived[1][None],
        up_weight_grad[None],
        bias_grad,
        down_weight_grad[None],
        down_bias_grad[None],
        params[0][None],
        params[1][None],
    )


def solution(mesh):
    names = ("section", "dp", "z", "xh", "core")
    split = Mesh(mesh.devices.reshape(2, 4, 8, 2, 2), names)
    mp = ("z", "xh", "core")
    specs = (
        P("section", mp, "dp"),
        P("section", mp, "dp"),
        P("section", mp, "dp"),
        P("section", "dp"),
        P("section", "dp"),
        P("section", "dp", mp),
        P("section", mp),
        P("section", mp, "dp"),
        P("section", "dp"),
    )
    return jax.shard_map(
        local,
        mesh=split,
        in_specs=specs,
        out_specs=(
            P("section", None, ("dp",) + mp),
            P("section", None, ("dp",) + mp),
            P("section", "dp", mp),
            P("section", mp),
            P("section", mp, "dp"),
            P("section", "dp"),
            P("section", "dp"),
            P("section", "dp"),
        ),
        check_vma=False,
    )
```

```python
import jax
import jax.numpy as jnp
from jax import lax
from jax.experimental import pallas as pl
from jax.experimental.pallas import tpu as pltpu
from jax.sharding import Mesh, PartitionSpec as P

D = 8192


EPS = 1e-05
COEF_A = 0.7978845608028654
COEF_B = 0.044715
F32 = jnp.float32
BF = jnp.bfloat16


def shifted(value, axis, steps):
    count = lax.axis_size(axis)
    return lax.ppermute(value, axis, [(i, (i + steps) % count) for i in range(count)])


def swapped(value, axis, bit):
    count = lax.axis_size(axis)
    return lax.ppermute(value, axis, [(i, i ^ bit) for i in range(count)])


def gelu_value(value):
    inner = jnp.tanh(COEF_A * (value + COEF_B * value * value * value))
    return 0.5 * value * (1.0 + inner)


def gelu_slope(value):
    inner = jnp.tanh(COEF_A * (value + COEF_B * value * value * value))
    return 0.5 * (1.0 + inner) + 0.5 * value * (1.0 - inner * inner) * COEF_A * (
        1.0 + 3.0 * COEF_B * value * value
    )


def take(value, index, axis):
    return lax.dynamic_index_in_dim(value, index, axis, keepdims=False)


def over_dp(value):
    return value + shifted(value, "dp", 1) + shifted(value, "dp", 2) + shifted(value, "dp", 3)


def gather_half(own):
    at_z, even = lax.axis_index("z"), lax.axis_index("xh") == 0
    other = swapped(own, "xh", 1)
    pair = jnp.where(even, jnp.stack([own, other], 1), jnp.stack([other, own], 1))
    whole = jnp.zeros((own.shape[0], 8) + pair.shape[1:], own.dtype)
    whole = lax.dynamic_update_index_in_dim(whole, pair, at_z, 1)
    ahead, behind = pair, pair
    for step in range(1, 5):
        ahead = shifted(ahead, "z", 1)
        if step < 4:
            behind = shifted(behind, "z", -1)
            whole = lax.dynamic_update_index_in_dim(whole, behind, (at_z + step) % 8, 1)
        whole = lax.dynamic_update_index_in_dim(whole, ahead, (at_z + 8 - step) % 8, 1)
    return whole.reshape(own.shape[0], 128, own.shape[2])


def together_kernel(a, b, c, whole):
    for i, part in enumerate((a, b, c)):
        whole[i] = part[0]


def together(a, b, c):
    return pl.pallas_call(
        together_kernel,
        out_shape=jax.ShapeDtypeStruct((3,) + a.shape[1:], a.dtype),
        name="together",
    )(a, b, c)


def fetched_kernel(far_up, far_down, near_up, near_down, arrived):
    copies = [
        pltpu.make_async_copy(far_up, near_up, arrived.at[0]),
        pltpu.make_async_copy(far_down, near_down, arrived.at[1]),
    ]
    for copy in copies:
        copy.start()
    for copy in copies:
        copy.wait()


def fetched(w_up, w_down):
    return pl.pallas_call(
        fetched_kernel,
        in_specs=[pl.BlockSpec(memory_space=pltpu.HBM)] * 2,
        out_specs=[pl.BlockSpec(memory_space=pltpu.VMEM)] * 2,
        out_shape=[jax.ShapeDtypeStruct(w.shape, w.dtype) for w in (w_up, w_down)],
        scratch_shapes=[pltpu.SemaphoreType.DMA((2,))],
        compiler_params=pltpu.CompilerParams(vmem_limit_bytes=8 * 2**20),
        cost_estimate=pl.CostEstimate(flops=0, bytes_accessed=8 * 2**20, transcendentals=0),
        name="fetched",
    )(w_up, w_down)


def in_thirds(value):
    high = value.astype(BF).astype(F32)
    rest = value - high
    middle = rest.astype(BF).astype(F32)
    return high, middle, rest - middle


def entry_kernel(
    at_dp, mine, other, gain, shift, w_up, w_down,
    sent0, sent1, sent2, sent3, scaled, grads, rows, extra, turned, found,
):
    width = mine.shape[2]
    extra[...] = jnp.zeros_like(extra)
    rows[...] = jnp.zeros_like(rows)
    lane = lax.broadcasted_iota(jnp.int32, (128, 128), 1)
    for half, tokens in enumerate((mine, other)):
        columns = jnp.zeros((128, 128), F32)
        for i in range(2):
            value = tokens[i].astype(F32)
            total = jnp.sum(value, 1, keepdims=True)
            square = jnp.sum(value * value, 1, keepdims=True)
            columns = jnp.where(lane == 2 * i, total, columns)
            columns = jnp.where(lane == 2 * i + 1, square, columns)
            scaled[i, half * 128 : half * 128 + 128, :] = (
                (value - total / width) * gain[...]
            ).astype(BF)
        turned[...] = columns.T
        grads[half * 128 : half * 128 + 128, :] = tokens[2]
        for k, third in enumerate(in_thirds(turned[0:4, :])):
            extra[6 + 4 * half : 10 + 4 * half, k * 128 : k * 128 + 128] = third
    for j, vector in enumerate((gain, shift)):
        for k, third in enumerate(in_thirds(vector[...])):
            rows[3 * j + k : 3 * j + k + 1, :] = third
    sums = jnp.dot(rows[...].astype(BF), w_up[...], preferred_element_type=F32)
    for j in range(2):
        vector = sums[3 * j : 3 * j + 1] + sums[3 * j + 1 : 3 * j + 2] + sums[3 * j + 2 : 3 * j + 3]
        for k, third in enumerate(in_thirds(vector)):
            extra[3 * j + k : 3 * j + k + 1, :] = third
    for i in range(2):
        found[i] = jnp.dot(scaled[i], w_up[...], preferred_element_type=F32).astype(BF)
    found[2] = lax.dot_general(
        grads[...], w_down[...], (((1,), (1,)), ((), ())), preferred_element_type=F32
    ).astype(BF)
    for k, sent in enumerate((sent0, sent1, sent2, sent3)):
        row = pl.multiple_of(((at_dp[0] + k) % 4) * 64, 64)
        for i in range(3):
            sent[64 * i : 64 * i + 64, :] = found[i, pl.ds(row, 64), :]
        sent[192:208, :] = extra[...].astype(BF)


def entry(mine, other, gain, shift, w_up, w_down):
    return pl.pallas_call(
        entry_kernel,
        in_specs=[pl.BlockSpec(memory_space=pltpu.SMEM)]
        + [pl.BlockSpec(memory_space=pltpu.VMEM)] * 6,
        out_specs=[pl.BlockSpec(memory_space=pltpu.VMEM)] * 4,
        out_shape=[jax.ShapeDtypeStruct((208, 512), BF)] * 4,
        scratch_shapes=[
            pltpu.VMEM((2, 256, 2048), BF),
            pltpu.VMEM((256, 2048), BF),
            pltpu.VMEM((8, 2048), F32),
            pltpu.VMEM((16, 512), F32),
            pltpu.VMEM((128, 128), F32),
            pltpu.VMEM((3, 256, 512), BF),
        ],
        compiler_params=pltpu.CompilerParams(vmem_limit_bytes=28 * 2**20),
        cost_estimate=pl.CostEstimate(
            flops=2**31, bytes_accessed=8 * 2**20, transcendentals=0
        ),
        name="entry",
    )(lax.axis_index("dp").reshape(1), mine, other, gain, shift, w_up, w_down)


def middle_kernel(at_dp, part0, part1, part2, part3, bias, quarter, stats, rows):
    parts = (part0, part1, part2, part3)
    extra = jnp.stack([part[192:208, :].astype(F32) for part in parts])
    weights = [
        [extra[y, 3 * j : 3 * j + 1] + extra[y, 3 * j + 1 : 3 * j + 2] + extra[y, 3 * j + 2 : 3 * j + 3] for y in range(4)]
        for j in range(2)
    ]
    offset = weights[1][0] + weights[1][1] + weights[1][2] + weights[1][3] + bias[...]
    rows[...] = jnp.zeros_like(rows)
    for half in range(2):
        block = extra[:, 6 + 4 * half : 10 + 4 * half, :]
        sums = block[:, :, 0:128] + block[:, :, 128:256] + block[:, :, 256:384]
        whole = sums[0] + sums[1] + sums[2] + sums[3]
        for i in range(2):
            mean = whole[2 * i : 2 * i + 1] / D
            square = whole[2 * i + 1 : 2 * i + 2] / D
            rows[2 * i : 2 * i + 1, :] = mean
            rows[2 * i + 1 : 2 * i + 2, :] = lax.rsqrt(square - mean * mean + EPS)
            for y in range(4):
                at = 4 + 4 * i + y
                rows[at : at + 1, :] = sums[y, 2 * i : 2 * i + 1] / (D // 4) - mean
        stats[half * 128 : half * 128 + 128, :] = rows[...].T
    own = stats[pl.ds(pl.multiple_of(at_dp[0] * 64, 64), 64), :]
    for i in range(2):
        total = jnp.zeros((64, 512), F32)
        for y in range(4):
            at = 4 + 4 * i + y
            total += parts[y][64 * i : 64 * i + 64, :].astype(F32)
            total += own[:, at : at + 1] * weights[0][y]
        pre = own[:, 2 * i + 1 : 2 * i + 2] * total + offset
        quarter[i] = gelu_value(pre).astype(BF)
    back = parts[0][128:192, :].astype(F32)
    for y in range(1, 4):
        back += parts[y][128:192, :].astype(F32)
    quarter[2] = (back * gelu_slope(pre)).astype(BF)


def middle(parts, bias):
    return pl.pallas_call(
        middle_kernel,
        in_specs=[pl.BlockSpec(memory_space=pltpu.SMEM)]
        + [pl.BlockSpec(memory_space=pltpu.VMEM)] * 5,
        out_specs=[pl.BlockSpec(memory_space=pltpu.VMEM)] * 2,
        out_shape=[
            jax.ShapeDtypeStruct((3, 64, 512), BF),
            jax.ShapeDtypeStruct((256, 128), F32),
        ],
        scratch_shapes=[pltpu.VMEM((128, 128), F32)],
        compiler_params=pltpu.CompilerParams(vmem_limit_bytes=12 * 2**20),
        cost_estimate=pl.CostEstimate(
            flops=2**22, bytes_accessed=2**20, transcendentals=2**17
        ),
        name="middle",
    )(lax.axis_index("dp").reshape(1), *parts, bias)


def products_kernel(
    at_dp, own, next1, next2, next3, far_up, far_down, mine, other, stats, gain,
    kept, given, hidden, bias_grad, params, moments, w_up, w_down, arrived,
):
    copies = []
    for part in range(4):
        block = slice(part * 512, part * 512 + 512)
        copies.append((
            pltpu.make_async_copy(far_down.at[:, block], w_down.at[:, block], arrived.at[0, part]),
            pltpu.make_async_copy(far_up.at[block], w_up.at[block], arrived.at[1, part]),
        ))
        for copy in copies[-1]:
            copy.start()
    for k, quarter in enumerate((own, next1, next2, next3)):
        row = pl.multiple_of(((at_dp[0] + k) % 4) * 64, 64)
        for i in range(3):
            hidden[i, pl.ds(row, 64), :] = quarter[i]
    bias_grad[...] = jnp.sum(hidden[2].astype(F32), 0, keepdims=True)
    plain = jnp.zeros((256, 128), F32)
    crossed = jnp.zeros((256, 128), F32)
    for z in range(8):
        columns = slice(z * 256, z * 256 + 256)
        if z % 2 == 0:
            for copy in copies[z // 2]:
                copy.wait()
        branch = jnp.dot(hidden[0], w_down[:, columns], preferred_element_type=F32)
        back = lax.dot_general(
            hidden[2], w_up[columns, :], (((1,), (1,)), ((), ())), preferred_element_type=F32
        )
        for h in range(2):
            lanes = slice(h * 128, h * 128 + 128)
            for i, product in enumerate((branch, back)):
                kept[z, h, i] = product[:128, lanes]
                given[z, h, i] = product[128:, lanes].astype(BF)
        saved = jnp.concatenate([mine[1, :, columns], other[1, :, columns]]).astype(F32)
        centered = (saved - stats[:, 2:3]) * stats[:, 3:4]
        crossing = back * centered
        params[0:1, columns] = jnp.sum(crossing, 0, keepdims=True)
        params[1:2, columns] = jnp.sum(back, 0, keepdims=True)
        weighed, crossing = back * gain[:, columns], crossing * gain[:, columns]
        plain += weighed[:, :128] + weighed[:, 128:]
        crossed += crossing[:, :128] + crossing[:, 128:]
    ones = jnp.ones((8, 128), F32)
    for i, total in enumerate((plain, crossed)):
        row = lax.dot_general(
            ones, total, (((1,), (1,)), ((), ())),
            precision=lax.Precision.HIGHEST, preferred_element_type=F32,
        )
        moments[i : i + 1, :] = row[0:1]


def products(quarters, w_up, w_down, mine, other, stats, gain):
    out = lambda shape, kind: jax.ShapeDtypeStruct(shape, kind)
    return pl.pallas_call(
        products_kernel,
        in_specs=[pl.BlockSpec(memory_space=pltpu.SMEM)]
        + [pl.BlockSpec(memory_space=pltpu.VMEM)] * 4
        + [pl.BlockSpec(memory_space=pltpu.HBM)] * 2
        + [pl.BlockSpec(memory_space=pltpu.VMEM)] * 4,
        out_specs=[pl.BlockSpec(memory_space=pltpu.VMEM)] * 6,
        out_shape=[
            out((8, 2, 2, 128, 128), F32),
            out((8, 2, 2, 128, 128), BF),
            out((3, 256, 512), BF),
            out((1, 512), F32),
            out((2, 2048), F32),
            out((2, 256), F32),
        ],
        scratch_shapes=[
            pltpu.VMEM((2048, 512), BF),
            pltpu.VMEM((512, 2048), BF),
            pltpu.SemaphoreType.DMA((2, 4)),
        ],
        compiler_params=pltpu.CompilerParams(vmem_limit_bytes=46 * 2**20),
        cost_estimate=pl.CostEstimate(
            flops=2**31, bytes_accessed=10 * 2**20, transcendentals=0
        ),
        name="products",
    )(lax.axis_index("dp").reshape(1), *quarters, w_up, w_down, mine, other, stats, gain)


def relayed(tiles):
    count = tiles.shape[0]
    even = lax.axis_index("core") == 0
    low, high = tiles[:, :, :64], tiles[:, :, 64:]
    same = swapped(jnp.where(even, low, high), "section", 1)
    cross = lax.ppermute(jnp.where(even, high, low), ("section", "core"), [(i, 3 - i) for i in range(4)])
    same, cross = same.reshape(count, 16, 8, 64), cross.reshape(count, 16, 8, 64)
    joined = jnp.where(even, jnp.stack([same, cross], 2), jnp.stack([cross, same], 2))
    return joined.reshape(count, 256, 64)


def local(
    section_input,
    saved_input,
    cotangent,
    norm_gain,
    norm_shift,
    up_weight,
    up_bias,
    down_weight,
    down_bias,
):
    gain, shift = (norm_gain[0], norm_shift[0])
    w_up, w_down = (up_weight[0], down_weight[0])
    bias_up, bias_down = (up_bias[0], down_bias[0])
    at_z, at_h = (lax.axis_index("z"), lax.axis_index("xh"))
    first_column = at_z * 256 + at_h * 128

    mine = gather_half(together(section_input, saved_input, cotangent))
    other = swapped(mine, "core", 1)

    near_up, near_down = fetched(w_up, w_down)
    parts = entry(mine, other, gain[None], shift[None], near_up, near_down)
    parts = [parts[0]] + [shifted(parts[k], "dp", k) for k in (1, 2, 3)]
    quarter, stats = middle(parts, bias_up[None])
    quarters = [quarter] + [shifted(quarter, "dp", -k) for k in (1, 2, 3)]

    kept, given, hidden, bias_grad, params, moments = products(
        quarters, w_up, w_down, mine, other, stats, gain[None]
    )
    summed = kept + swapped(given, "core", 1).astype(F32)
    given = take(summed, 1 - at_h, 1).astype(BF)
    small = jnp.concatenate([moments, params], 1)
    kept = take(summed, at_h, 1) + swapped(given, "xh", 1).astype(F32)
    for bit in (1, 2, 4):
        small = small + swapped(small, "z", bit)
    grad_full = jnp.concatenate([mine[2], other[2]])
    saved = jnp.concatenate([mine[1], other[1]]).astype(F32)
    normed = ((saved - stats[:, 2:3]) * stats[:, 3:4] * gain + shift).astype(BF)
    down_weight_grad = lax.dot_general(
        hidden[1], grad_full, (((0,), (0,)), ((), ())), preferred_element_type=F32
    ).astype(BF)
    down_bias_grad = jnp.sum(grad_full.astype(F32), 0)
    up_weight_grad = lax.dot_general(
        normed, hidden[2], (((0,), (0,)), ((), ())), preferred_element_type=F32
    ).astype(BF)
    kept, up_weight_grad, down_weight_grad = lax.optimization_barrier(
        (kept.astype(BF), up_weight_grad, down_weight_grad)
    )
    tiles = jnp.sum(lax.all_to_all(kept, "z", 0, 0, tiled=False).astype(F32), 0)
    small = jnp.concatenate([small[:, :128], small[:, 256:]], 1) + swapped(
        small[:, 128:], "core", 1
    )
    small = small + swapped(small, "xh", 1)
    small = jnp.concatenate([over_dp(small[:, :128]), small[:, 128:]], 1)
    moments, params = small[:, :128], small[:, 128:]

    def own_tile(value):
        return lax.dynamic_slice_in_dim(value, first_column, 128, 1).astype(F32)

    def own_columns(vector):
        return lax.dynamic_slice_in_dim(vector, first_column, 128, 0)

    out = (own_tile(mine[0]) + tiles[0] + own_columns(bias_down)).astype(BF)

    rstd_rows = stats[:128, 3:4]
    centered_tile = (own_tile(mine[1]) - stats[:128, 2:3]) * rstd_rows
    first, second = moments[0][:, None] / D, moments[1][:, None] / D
    grad_in = own_tile(mine[2]) + rstd_rows * (
        tiles[1] * own_columns(gain) - first - centered_tile * second
    )
    arrived = relayed(jnp.stack([out, grad_in.astype(BF)]))

    return (
        arrived[0][None],
        arrived[1][None],
        up_weight_grad[None],
        bias_grad,
        down_weight_grad[None],
        down_bias_grad[None],
        params[0][None],
        params[1][None],
    )


def solution(mesh):
    names = ("section", "dp", "z", "xh", "core")
    split = Mesh(mesh.devices.reshape(2, 4, 8, 2, 2), names)
    mp = ("z", "xh", "core")
    specs = (
        P("section", mp, "dp"),
        P("section", mp, "dp"),
        P("section", mp, "dp"),
        P("section", "dp"),
        P("section", "dp"),
        P("section", "dp", mp),
        P("section", mp),
        P("section", mp, "dp"),
        P("section", "dp"),
    )
    return jax.shard_map(
        local,
        mesh=split,
        in_specs=specs,
        out_specs=(
            P("section", None, ("dp",) + mp),
            P("section", None, ("dp",) + mp),
            P("section", "dp", mp),
            P("section", mp),
            P("section", mp, "dp"),
            P("section", "dp"),
            P("section", "dp"),
            P("section", "dp"),
        ),
        check_vma=False,
    )
```

```python
import jax
import jax.numpy as jnp
from jax import lax
from jax.experimental import pallas as pl
from jax.experimental.pallas import tpu as pltpu
from jax.sharding import Mesh, PartitionSpec as P

D = 8192


EPS = 1e-05
COEF_A = 0.7978845608028654
COEF_B = 0.044715
F32 = jnp.float32
BF = jnp.bfloat16


def shifted(value, axis, steps):
    count = lax.axis_size(axis)
    return lax.ppermute(value, axis, [(i, (i + steps) % count) for i in range(count)])


def swapped(value, axis, bit):
    count = lax.axis_size(axis)
    return lax.ppermute(value, axis, [(i, i ^ bit) for i in range(count)])


def gelu_value(value):
    inner = jnp.tanh(COEF_A * (value + COEF_B * value * value * value))
    return 0.5 * value * (1.0 + inner)


def gelu_slope(value):
    inner = jnp.tanh(COEF_A * (value + COEF_B * value * value * value))
    return 0.5 * (1.0 + inner) + 0.5 * value * (1.0 - inner * inner) * COEF_A * (
        1.0 + 3.0 * COEF_B * value * value
    )


def take(value, index, axis):
    return lax.dynamic_index_in_dim(value, index, axis, keepdims=False)


def over_dp(value):
    return value + shifted(value, "dp", 1) + shifted(value, "dp", 2) + shifted(value, "dp", 3)


def gather_half(own):
    at_z, even = lax.axis_index("z"), lax.axis_index("xh") == 0
    other = swapped(own, "xh", 1)
    pair = jnp.where(even, jnp.stack([own, other], 1), jnp.stack([other, own], 1))
    whole = jnp.zeros((own.shape[0], 8) + pair.shape[1:], own.dtype)
    whole = lax.dynamic_update_index_in_dim(whole, pair, at_z, 1)
    ahead, behind = pair, pair
    for step in range(1, 5):
        ahead = shifted(ahead, "z", 1)
        if step < 4:
            behind = shifted(behind, "z", -1)
            whole = lax.dynamic_update_index_in_dim(whole, behind, (at_z + step) % 8, 1)
        whole = lax.dynamic_update_index_in_dim(whole, ahead, (at_z + 8 - step) % 8, 1)
    return whole.reshape(own.shape[0], 128, own.shape[2])


def together_kernel(a, b, c, whole):
    for i, part in enumerate((a, b, c)):
        whole[i] = part[0]


def together(a, b, c):
    return pl.pallas_call(
        together_kernel,
        out_shape=jax.ShapeDtypeStruct((3,) + a.shape[1:], a.dtype),
        name="together",
    )(a, b, c)


def in_thirds(value):
    high = value.astype(BF).astype(F32)
    rest = value - high
    middle = rest.astype(BF).astype(F32)
    return high, middle, rest - middle


def half_products(half, tokens, gain, w_up, w_down, found, scaled, extra, turned):
    width = tokens.shape[2]
    lane = lax.broadcasted_iota(jnp.int32, (128, 128), 1)
    columns = jnp.zeros((128, 128), F32)
    for i in range(2):
        value = tokens[i].astype(F32)
        total = jnp.sum(value, 1, keepdims=True)
        square = jnp.sum(value * value, 1, keepdims=True)
        columns = jnp.where(lane == 2 * i, total, columns)
        columns = jnp.where(lane == 2 * i + 1, square, columns)
        scaled[i * 128 : i * 128 + 128, :] = ((value - total / width) * gain[...]).astype(BF)
    turned[...] = columns.T
    for k, third in enumerate(in_thirds(turned[0:4, :])):
        extra[6 + 4 * half : 10 + 4 * half, k * 128 : k * 128 + 128] = third
    rows = slice(half * 128, half * 128 + 128)
    product = jnp.dot(scaled[...], w_up[...], preferred_element_type=F32).astype(BF)
    for i in range(2):
        found[i, rows, :] = product[i * 128 : i * 128 + 128]
    found[2, rows, :] = lax.dot_general(
        tokens[2], w_down[...], (((1,), (1,)), ((), ())), preferred_element_type=F32
    ).astype(BF)


def first_kernel(
    mine, gain, shift, far_up, far_down, found, extra, w_up, w_down, scaled, rows, turned, arrived
):
    copies = [
        pltpu.make_async_copy(far_up, w_up, arrived.at[0]),
        pltpu.make_async_copy(far_down, w_down, arrived.at[1]),
    ]
    for copy in copies:
        copy.start()
    extra[...] = jnp.zeros_like(extra)
    rows[...] = jnp.zeros_like(rows)
    for j, vector in enumerate((gain, shift)):
        for k, third in enumerate(in_thirds(vector[...])):
            rows[3 * j + k : 3 * j + k + 1, :] = third
    for copy in copies:
        copy.wait()
    sums = jnp.dot(rows[...].astype(BF), w_up[...], preferred_element_type=F32)
    for j in range(2):
        vector = sums[3 * j : 3 * j + 1] + sums[3 * j + 1 : 3 * j + 2] + sums[3 * j + 2 : 3 * j + 3]
        for k, third in enumerate(in_thirds(vector)):
            extra[3 * j + k : 3 * j + k + 1, :] = third
    half_products(0, mine, gain, w_up, w_down, found, scaled, extra, turned)


def second_kernel(
    at_dp, found0, extra0, other, gain, w_up, w_down,
    sent0, sent1, sent2, sent3, scaled, extra, turned, found,
):
    extra[...] = extra0[...]
    for i in range(3):
        found[i, 0:128, :] = found0[i]
    half_products(1, other, gain, w_up, w_down, found, scaled, extra, turned)
    for k, sent in enumerate((sent0, sent1, sent2, sent3)):
        row = pl.multiple_of(((at_dp[0] + k) % 4) * 64, 64)
        for i in range(3):
            sent[64 * i : 64 * i + 64, :] = found[i, pl.ds(row, 64), :]
        sent[192:208, :] = extra[...].astype(BF)


def entry(mine, other, gain, shift, w_up, w_down):
    held = pl.BlockSpec(memory_space=pltpu.VMEM)
    params = pltpu.CompilerParams(vmem_limit_bytes=20 * 2**20)
    cost = pl.CostEstimate(flops=2**30, bytes_accessed=4 * 2**20, transcendentals=0)
    found, extra, w_up, w_down = pl.pallas_call(
        first_kernel,
        in_specs=[held] * 3 + [pl.BlockSpec(memory_space=pltpu.HBM)] * 2,
        out_specs=[held] * 4,
        out_shape=[
            jax.ShapeDtypeStruct((3, 128, 512), BF),
            jax.ShapeDtypeStruct((16, 512), F32),
            jax.ShapeDtypeStruct((2048, 512), BF),
            jax.ShapeDtypeStruct((512, 2048), BF),
        ],
        scratch_shapes=[
            pltpu.VMEM((256, 2048), BF),
            pltpu.VMEM((8, 2048), F32),
            pltpu.VMEM((128, 128), F32),
            pltpu.SemaphoreType.DMA((2,)),
        ],
        compiler_params=pltpu.CompilerParams(vmem_limit_bytes=50 * 2**20),
        cost_estimate=cost,
        name="first_half",
    )(mine, gain, shift, w_up, w_down)
    return pl.pallas_call(
        second_kernel,
        in_specs=[pl.BlockSpec(memory_space=pltpu.SMEM)] + [held] * 6,
        out_specs=[held] * 4,
        out_shape=[jax.ShapeDtypeStruct((208, 512), BF)] * 4,
        scratch_shapes=[
            pltpu.VMEM((256, 2048), BF),
            pltpu.VMEM((16, 512), F32),
            pltpu.VMEM((128, 128), F32),
            pltpu.VMEM((3, 256, 512), BF),
        ],
        compiler_params=params,
        cost_estimate=cost,
        name="second_half",
    )(lax.axis_index("dp").reshape(1), found, extra, other, gain, w_up, w_down)


def middle_kernel(at_dp, part0, part1, part2, part3, bias, quarter, stats, rows):
    parts = (part0, part1, part2, part3)
    extra = jnp.stack([part[192:208, :].astype(F32) for part in parts])
    weights = [
        [extra[y, 3 * j : 3 * j + 1] + extra[y, 3 * j + 1 : 3 * j + 2] + extra[y, 3 * j + 2 : 3 * j + 3] for y in range(4)]
        for j in range(2)
    ]
    offset = weights[1][0] + weights[1][1] + weights[1][2] + weights[1][3] + bias[...]
    rows[...] = jnp.zeros_like(rows)
    for half in range(2):
        block = extra[:, 6 + 4 * half : 10 + 4 * half, :]
        sums = block[:, :, 0:128] + block[:, :, 128:256] + block[:, :, 256:384]
        whole = sums[0] + sums[1] + sums[2] + sums[3]
        for i in range(2):
            mean = whole[2 * i : 2 * i + 1] / D
            square = whole[2 * i + 1 : 2 * i + 2] / D
            rows[2 * i : 2 * i + 1, :] = mean
            rows[2 * i + 1 : 2 * i + 2, :] = lax.rsqrt(square - mean * mean + EPS)
            for y in range(4):
                at = 4 + 4 * i + y
                rows[at : at + 1, :] = sums[y, 2 * i : 2 * i + 1] / (D // 4) - mean
        stats[half * 128 : half * 128 + 128, :] = rows[...].T
    own = stats[pl.ds(pl.multiple_of(at_dp[0] * 64, 64), 64), :]
    for i in range(2):
        total = jnp.zeros((64, 512), F32)
        for y in range(4):
            at = 4 + 4 * i + y
            total += parts[y][64 * i : 64 * i + 64, :].astype(F32)
            total += own[:, at : at + 1] * weights[0][y]
        pre = own[:, 2 * i + 1 : 2 * i + 2] * total + offset
        quarter[i] = gelu_value(pre).astype(BF)
    back = parts[0][128:192, :].astype(F32)
    for y in range(1, 4):
        back += parts[y][128:192, :].astype(F32)
    quarter[2] = (back * gelu_slope(pre)).astype(BF)


def middle(parts, bias):
    return pl.pallas_call(
        middle_kernel,
        in_specs=[pl.BlockSpec(memory_space=pltpu.SMEM)]
        + [pl.BlockSpec(memory_space=pltpu.VMEM)] * 5,
        out_specs=[pl.BlockSpec(memory_space=pltpu.VMEM)] * 2,
        out_shape=[
            jax.ShapeDtypeStruct((3, 64, 512), BF),
            jax.ShapeDtypeStruct((256, 128), F32),
        ],
        scratch_shapes=[pltpu.VMEM((128, 128), F32)],
        compiler_params=pltpu.CompilerParams(vmem_limit_bytes=12 * 2**20),
        cost_estimate=pl.CostEstimate(
            flops=2**22, bytes_accessed=2**20, transcendentals=2**17
        ),
        name="middle",
    )(lax.axis_index("dp").reshape(1), *parts, bias)


def products_kernel(
    at_dp, own, next1, next2, next3, far_up, far_down, mine, other, stats, gain,
    kept, given, hidden, bias_grad, params, moments, w_up, w_down, arrived,
):
    copies = []
    for part in range(4):
        block = slice(part * 512, part * 512 + 512)
        copies.append((
            pltpu.make_async_copy(far_down.at[:, block], w_down.at[:, block], arrived.at[0, part]),
            pltpu.make_async_copy(far_up.at[block], w_up.at[block], arrived.at[1, part]),
        ))
        for copy in copies[-1]:
            copy.start()
    for k, quarter in enumerate((own, next1, next2, next3)):
        row = pl.multiple_of(((at_dp[0] + k) % 4) * 64, 64)
        for i in range(3):
            hidden[i, pl.ds(row, 64), :] = quarter[i]
    bias_grad[...] = jnp.sum(hidden[2].astype(F32), 0, keepdims=True)
    plain = jnp.zeros((256, 128), F32)
    crossed = jnp.zeros((256, 128), F32)
    for z in range(8):
        columns = slice(z * 256, z * 256 + 256)
        if z % 2 == 0:
            for copy in copies[z // 2]:
                copy.wait()
        branch = jnp.dot(hidden[0], w_down[:, columns], preferred_element_type=F32)
        back = lax.dot_general(
            hidden[2], w_up[columns, :], (((1,), (1,)), ((), ())), preferred_element_type=F32
        )
        for h in range(2):
            lanes = slice(h * 128, h * 128 + 128)
            for i, product in enumerate((branch, back)):
                kept[z, h, i] = product[:128, lanes]
                given[z, h, i] = product[128:, lanes].astype(BF)
        saved = jnp.concatenate([mine[1, :, columns], other[1, :, columns]]).astype(F32)
        centered = (saved - stats[:, 2:3]) * stats[:, 3:4]
        crossing = back * centered
        params[0:1, columns] = jnp.sum(crossing, 0, keepdims=True)
        params[1:2, columns] = jnp.sum(back, 0, keepdims=True)
        weighed, crossing = back * gain[:, columns], crossing * gain[:, columns]
        plain += weighed[:, :128] + weighed[:, 128:]
        crossed += crossing[:, :128] + crossing[:, 128:]
    ones = jnp.ones((8, 128), F32)
    for i, total in enumerate((plain, crossed)):
        row = lax.dot_general(
            ones, total, (((1,), (1,)), ((), ())),
            precision=lax.Precision.HIGHEST, preferred_element_type=F32,
        )
        moments[i : i + 1, :] = row[0:1]


def products(quarters, w_up, w_down, mine, other, stats, gain):
    out = lambda shape, kind: jax.ShapeDtypeStruct(shape, kind)
    return pl.pallas_call(
        products_kernel,
        in_specs=[pl.BlockSpec(memory_space=pltpu.SMEM)]
        + [pl.BlockSpec(memory_space=pltpu.VMEM)] * 4
        + [pl.BlockSpec(memory_space=pltpu.HBM)] * 2
        + [pl.BlockSpec(memory_space=pltpu.VMEM)] * 4,
        out_specs=[pl.BlockSpec(memory_space=pltpu.VMEM)] * 6,
        out_shape=[
            out((8, 2, 2, 128, 128), F32),
            out((8, 2, 2, 128, 128), BF),
            out((3, 256, 512), BF),
            out((1, 512), F32),
            out((2, 2048), F32),
            out((2, 256), F32),
        ],
        scratch_shapes=[
            pltpu.VMEM((2048, 512), BF),
            pltpu.VMEM((512, 2048), BF),
            pltpu.SemaphoreType.DMA((2, 4)),
        ],
        compiler_params=pltpu.CompilerParams(vmem_limit_bytes=46 * 2**20),
        cost_estimate=pl.CostEstimate(
            flops=2**31, bytes_accessed=10 * 2**20, transcendentals=0
        ),
        name="products",
    )(lax.axis_index("dp").reshape(1), *quarters, w_up, w_down, mine, other, stats, gain)


def relayed(tiles):
    count = tiles.shape[0]
    even = lax.axis_index("core") == 0
    low, high = tiles[:, :, :64], tiles[:, :, 64:]
    same = swapped(jnp.where(even, low, high), "section", 1)
    cross = lax.ppermute(jnp.where(even, high, low), ("section", "core"), [(i, 3 - i) for i in range(4)])
    same, cross = same.reshape(count, 16, 8, 64), cross.reshape(count, 16, 8, 64)
    joined = jnp.where(even, jnp.stack([same, cross], 2), jnp.stack([cross, same], 2))
    return joined.reshape(count, 256, 64)


def local(
    section_input,
    saved_input,
    cotangent,
    norm_gain,
    norm_shift,
    up_weight,
    up_bias,
    down_weight,
    down_bias,
):
    gain, shift = (norm_gain[0], norm_shift[0])
    w_up, w_down = (up_weight[0], down_weight[0])
    bias_up, bias_down = (up_bias[0], down_bias[0])
    at_z, at_h = (lax.axis_index("z"), lax.axis_index("xh"))
    first_column = at_z * 256 + at_h * 128

    mine = gather_half(together(section_input, saved_input, cotangent))
    other = swapped(mine, "core", 1)

    parts = entry(mine, other, gain[None], shift[None], w_up, w_down)
    parts = [parts[0]] + [shifted(parts[k], "dp", k) for k in (1, 2, 3)]
    quarter, stats = middle(parts, bias_up[None])
    quarters = [quarter] + [shifted(quarter, "dp", -k) for k in (1, 2, 3)]

    kept, given, hidden, bias_grad, params, moments = products(
        quarters, w_up, w_down, mine, other, stats, gain[None]
    )
    summed = kept + swapped(given, "core", 1).astype(F32)
    given = take(summed, 1 - at_h, 1).astype(BF)
    small = jnp.concatenate([moments, params], 1)
    kept = take(summed, at_h, 1) + swapped(given, "xh", 1).astype(F32)
    for bit in (1, 2, 4):
        small = small + swapped(small, "z", bit)
    grad_full = jnp.concatenate([mine[2], other[2]])
    saved = jnp.concatenate([mine[1], other[1]]).astype(F32)
    normed = ((saved - stats[:, 2:3]) * stats[:, 3:4] * gain + shift).astype(BF)
    down_weight_grad = lax.dot_general(
        hidden[1], grad_full, (((0,), (0,)), ((), ())), preferred_element_type=F32
    ).astype(BF)
    down_bias_grad = jnp.sum(grad_full.astype(F32), 0)
    up_weight_grad = lax.dot_general(
        normed, hidden[2], (((0,), (0,)), ((), ())), preferred_element_type=F32
    ).astype(BF)
    kept, up_weight_grad, down_weight_grad = lax.optimization_barrier(
        (kept.astype(BF), up_weight_grad, down_weight_grad)
    )
    tiles = jnp.sum(lax.all_to_all(kept, "z", 0, 0, tiled=False).astype(F32), 0)
    small = jnp.concatenate([small[:, :128], small[:, 256:]], 1) + swapped(
        small[:, 128:], "core", 1
    )
    small = small + swapped(small, "xh", 1)
    small = jnp.concatenate([over_dp(small[:, :128]), small[:, 128:]], 1)
    moments, params = small[:, :128], small[:, 128:]

    def own_tile(value):
        return lax.dynamic_slice_in_dim(value, first_column, 128, 1).astype(F32)

    def own_columns(vector):
        return lax.dynamic_slice_in_dim(vector, first_column, 128, 0)

    out = (own_tile(mine[0]) + tiles[0] + own_columns(bias_down)).astype(BF)

    rstd_rows = stats[:128, 3:4]
    centered_tile = (own_tile(mine[1]) - stats[:128, 2:3]) * rstd_rows
    first, second = moments[0][:, None] / D, moments[1][:, None] / D
    grad_in = own_tile(mine[2]) + rstd_rows * (
        tiles[1] * own_columns(gain) - first - centered_tile * second
    )
    arrived = relayed(jnp.stack([out, grad_in.astype(BF)]))

    return (
        arrived[0][None],
        arrived[1][None],
        up_weight_grad[None],
        bias_grad,
        down_weight_grad[None],
        down_bias_grad[None],
        params[0][None],
        params[1][None],
    )


def solution(mesh):
    names = ("section", "dp", "z", "xh", "core")
    split = Mesh(mesh.devices.reshape(2, 4, 8, 2, 2), names)
    mp = ("z", "xh", "core")
    specs = (
        P("section", mp, "dp"),
        P("section", mp, "dp"),
        P("section", mp, "dp"),
        P("section", "dp"),
        P("section", "dp"),
        P("section", "dp", mp),
        P("section", mp),
        P("section", mp, "dp"),
        P("section", "dp"),
    )
    return jax.shard_map(
        local,
        mesh=split,
        in_specs=specs,
        out_specs=(
            P("section", None, ("dp",) + mp),
            P("section", None, ("dp",) + mp),
            P("section", "dp", mp),
            P("section", mp),
            P("section", mp, "dp"),
            P("section", "dp"),
            P("section", "dp"),
            P("section", "dp"),
        ),
        check_vma=False,
    )
```
